32 devices in a mesh: dp: 8 (over y, x, core), ind: 4 (over z).
Axes of the slice: x: 2, y: 2, z: 4, core: 2. Of those that a mesh axis runs over, the one named last changes fastest.
Arguments:
- x_points: float32 [3, 16384], P(None, 'dp'), may hold values from 0 to 1
- z_points: float32 [3, 16384], P(None, 'ind'), may hold values from 0 to 1
- length_scales: float32 [3], replicated, may hold values from 0.35 to 0.7
- dpsi_grad: float32 [16384, 16384], P('dp', 'ind'), may hold values from -0.625 to 0.625
- block_rows: int32 [8, 4, 6], P('dp', 'ind'), may hold values from 0 to 7, as said below
- block_cols: int32 [8, 4, 6], P('dp', 'ind'), may hold values from 0 to 15, as said below
- block_count: int32 [8, 4], P('dp', 'ind'), may hold values from 3 to 6, as said below
Outputs:
- dk_blocks: float32 [8, 4, 6, 256, 256], P('dp', 'ind')
- z_grad: float32 [3, 16384], P(None, 'ind')
- scale_grad: float32 [3], replicated
The draws below stay inside these ranges and needn't reach their ends.
Inputs may be any that keep to these rules, and one draw needn't show every extreme that they name: `block_rows`: within a tile the live slots lie in distinct row blocks, and the live slots of all tiles of one row group lie in at most 6 distinct row blocks; entries of unused slots carry no meaning. `block_cols`: entries of unused slots carry no meaning. `block_count`: some tile holds exactly 6 listed blocks in every draw.
All inputs are finite; a program needn't handle non-finite values.
Results may differ from the reference program's by a relative error of at most 0.0003.
Values sent between devices are 32-bit elements; how exact they have to be, the bound alone decides.
A program may use at most 128 MiB of HBM per device.

```python
import math
import jax
import jax.numpy as jnp
from jax import lax

Q = 3
M = 16384
BS = 256
RB_DEV = 8
ROW_GROUPS = 8
COL_GROUPS = 4
CB_DEV = 16
CAP = 6
N = 16384


def pattern_parts(key):
    tiles_total = ROW_GROUPS * COL_GROUPS
    row_scores = jax.random.randint(jax.random.fold_in(key, 101), (ROW_GROUPS, RB_DEV), 0, 1 << 20)
    row_scores = row_scores * RB_DEV + jnp.arange(RB_DEV, dtype=jnp.int32)[None, :]
    active = jnp.argsort(row_scores, axis=1)[:, :CAP].astype(jnp.int32)
    slot_scores = jax.random.randint(jax.random.fold_in(key, 102), (ROW_GROUPS, COL_GROUPS, CAP), 0, 1 << 20)
    slot_scores = slot_scores * CAP + jnp.arange(CAP, dtype=jnp.int32)[None, None, :]
    order = jnp.argsort(slot_scores, axis=2).astype(jnp.int32)
    spread = jnp.broadcast_to(active[:, None, :], (ROW_GROUPS, COL_GROUPS, CAP))
    rows = jnp.take_along_axis(spread, order, axis=2).astype(jnp.int32)
    cols = jax.random.randint(jax.random.fold_in(key, 103), (ROW_GROUPS, COL_GROUPS, CAP), 0, CB_DEV).astype(jnp.int32)
    lowest = CAP // 2
    counts = jax.random.randint(jax.random.fold_in(key, 104), (tiles_total,), lowest, CAP + 1)
    full_tile = jax.random.randint(jax.random.fold_in(key, 105), (), 0, tiles_total)
    low_tile = (full_tile + 1 + jax.random.randint(jax.random.fold_in(key, 106), (), 0, tiles_total - 1)) % tiles_total
    tile_ids = jnp.arange(tiles_total, dtype=jnp.int32)
    counts = jnp.where(tile_ids == full_tile, CAP, counts)
    counts = jnp.where(tile_ids == low_tile, lowest, counts).astype(jnp.int32)
    return (rows, cols, counts.reshape(ROW_GROUPS, COL_GROUPS))


def draw_block_rows(key, part):
    return pattern_parts(key)[0]


def draw_block_cols(key, part):
    return pattern_parts(key)[1]


def draw_block_count(key, part):
    return pattern_parts(key)[2]


def shard_levels(rng, shape, cuts, smallest, high):
    gain, own = 1.0, jax.random.fold_in(rng, 6)
    for position, shards_of in cuts:
        draws = jnp.exp(jax.random.uniform(jax.random.fold_in(own, position), (shards_of,), jnp.float32, smallest / len(cuts), high / len(cuts)))
        gain = gain * jnp.repeat(draws, shape[position] // shards_of).reshape([-1 if axis == position else 1 for axis in range(len(shape))])
    return gain


def normal_values(rng, extent, scale, bound, split=(), kind=jnp.bfloat16):
    values = jax.random.normal(rng, extent, jnp.float32) * scale
    if len(split) > 0:
        values = shard_levels(rng, extent, split, -0.22, 0.18) * values
    return jnp.clip(values, min=-bound, max=bound).astype(kind)


def setup_inputs(seed: int = 0) -> dict:
    streams_of = jax.random.split(jax.random.key(seed), 8)
    return {
        "x_points": jnp.clip(1.0 * jax.random.uniform(streams_of[0], (Q, N), jnp.float32) ** shard_levels(streams_of[0], (Q, N), ((1, 8),), -0.2, 0.2), 0.0, 1.0),
        "z_points": jnp.clip(1.0 * jax.random.uniform(streams_of[1], (Q, M), jnp.float32) ** shard_levels(streams_of[1], (Q, M), ((1, 4),), -0.2, 0.2), 0.0, 1.0),
        "length_scales": jnp.clip(jnp.exp(jax.random.uniform(streams_of[2], (Q,), jnp.float32, math.log(0.35), math.log(0.7))), 0.35, 0.7),
        "dpsi_grad": normal_values(streams_of[3], (M, M), 0.1, 0.625, ((0, 8), (1, 4)), jnp.float32),
        "block_rows": draw_block_rows(jax.random.fold_in(streams_of[7], 71), 0),
        "block_cols": draw_block_cols(jax.random.fold_in(streams_of[7], 71), 0),
        "block_count": draw_block_count(jax.random.fold_in(streams_of[7], 71), 0),
    }


def wendland(x_rows, z_cols, length_scales):
    dist_sq = jnp.zeros((x_rows.shape[1], z_cols.shape[1]), x_rows.dtype)
    for dim_q in range(x_rows.shape[0]):
        offset = (x_rows[dim_q][:, None] - z_cols[dim_q][None, :]) / length_scales[dim_q]
        dist_sq = dist_sq + offset * offset
    radius = jnp.sqrt(dist_sq)
    remain = jnp.maximum(1.0 - radius, 0.0)
    remain_cube = remain * remain * remain
    return (remain_cube * remain * (4.0 * radius + 1.0), -10.0 * remain_cube)

def reference(x_points, z_points, length_scales, dpsi_grad, block_rows, block_cols, block_count):
    highest = lax.Precision.HIGHEST
    float_type = x_points.dtype
    total_slots = ROW_GROUPS * COL_GROUPS * CAP
    total_blocks = COL_GROUPS * CB_DEV
    live_all = jnp.arange(CAP, dtype=jnp.int32)[None, None, :] < block_count[:, :, None]
    z_blocks = z_points.reshape(Q, total_blocks, BS)
    group_ids = jnp.arange(COL_GROUPS, dtype=jnp.int32)

    def one_slot(flat_index):
        row_group = flat_index // (COL_GROUPS * CAP)
        column_group = flat_index // CAP % COL_GROUPS
        slot_index = flat_index % CAP
        row_local = block_rows[row_group, column_group, slot_index]
        col_local = block_cols[row_group, column_group, slot_index]
        live_weight = live_all[row_group, column_group, slot_index].astype(float_type)
        row_start = ((row_group * RB_DEV + row_local) * BS).astype(jnp.int32)
        col_start = ((column_group * CB_DEV + col_local) * BS).astype(jnp.int32)
        x_rows = lax.dynamic_slice_in_dim(x_points, row_start, BS, 1)
        z_cols = lax.dynamic_slice_in_dim(z_points, col_start, BS, 1)
        matched = live_all[row_group] & (block_rows[row_group] == row_local)
        near_weight = jnp.any(matched, axis=1).astype(float_type)
        near_local = lax.optimization_barrier(jnp.sum(jnp.where(matched, block_cols[row_group], 0), axis=1)).astype(jnp.int32)
        near_blocks = (group_ids * CB_DEV + near_local).astype(jnp.int32)
        z_near = z_blocks[:, near_blocks, :].reshape(Q, COL_GROUPS * BS)
        kernel, _ = wendland(x_rows, z_near, length_scales)
        masked = kernel * jnp.repeat(near_weight, BS)[None, :]
        near_starts = (near_blocks * BS).astype(jnp.int32)

        def pick_tile(row_at):
            return lax.dynamic_slice(dpsi_grad, (row_at, col_start), (BS, BS))
        near_tiles = jax.vmap(pick_tile)(near_starts).reshape(COL_GROUPS * BS, BS)
        dk_block = jnp.dot(masked, near_tiles, precision=highest) * live_weight
        _, slopes = wendland(x_rows, z_cols, length_scales)
        grad_k = dk_block * slopes
        col_sum = lax.optimization_barrier(jnp.sum(grad_k, axis=0))
        x_weighted = jnp.dot(x_rows, grad_k, precision=highest)
        z_part = (-2.0 / (length_scales * length_scales))[:, None] * (x_weighted - z_cols * col_sum[None, :])
        scale_terms = []
        for dim_q in range(x_rows.shape[0]):
            offset = x_rows[dim_q][:, None] - z_cols[dim_q][None, :]
            scale_terms.append(jnp.sum(grad_k * offset * offset))
        cube_scale = length_scales * length_scales * length_scales
        scale_part = -2.0 / cube_scale * jnp.stack(scale_terms)
        onehot = (jnp.arange(total_blocks, dtype=jnp.int32) == (column_group * CB_DEV + col_local).astype(jnp.int32)).astype(float_type)
        return (dk_block, z_part, scale_part, onehot)
    dk_all, z_parts, scale_parts, onehots = lax.map(one_slot, jnp.arange(total_slots, dtype=jnp.int32))
    z_grad = jnp.einsum('sm,sqb->qmb', onehots, z_parts, precision=highest).reshape(x_points.shape[0], M)
    scale_grad = lax.optimization_barrier(jnp.sum(scale_parts, axis=0))
    return (dk_all.reshape(ROW_GROUPS, COL_GROUPS, CAP, BS, BS), z_grad, scale_grad)
```

```python
import functools

import jax
import jax.numpy as jnp
from jax import lax
from jax.experimental import pallas as pl
from jax.experimental.pallas import tpu as pltpu
from jax.sharding import PartitionSpec as P

M = 16384
BS = 256


def wendland(x_rows, z_cols, length_scales):
    dist_sq = jnp.zeros((x_rows.shape[1], z_cols.shape[1]), x_rows.dtype)
    for dim_q in range(x_rows.shape[0]):
        offset = (x_rows[dim_q][:, None] - z_cols[dim_q][None, :]) / length_scales[dim_q]
        dist_sq = dist_sq + offset * offset
    radius = jnp.sqrt(dist_sq)
    remain = jnp.maximum(1.0 - radius, 0.0)
    remain_cube = remain * remain * remain
    return (remain_cube * remain * (4.0 * radius + 1.0), -10.0 * remain_cube)


def peers_of(axis, stride):
    size = lax.axis_size(axis) // stride
    index = lax.axis_index(axis)
    me = index // stride
    lane = index % stride
    others = []
    for step in range(1, size):
        other = lax.rem(me + step, size)
        others.append((other, {axis: other * stride + lane}))
    return me, others


def exchange_kernel(axis, stride, same, in_ref, out_ref, send_sem, recv_sem, local_sem):
    me, others = peers_of(axis, stride)
    barrier = pltpu.get_barrier_semaphore()
    for _, target in others:
        pl.semaphore_signal(barrier, inc=1, device_id=target, device_id_type=pl.DeviceIdType.MESH)
    pl.semaphore_wait(barrier, len(others))
    copies = []
    for step, (other, target) in enumerate(others):
        copy = pltpu.make_async_remote_copy(
            src_ref=in_ref if same else in_ref.at[other],
            dst_ref=out_ref.at[me],
            send_sem=send_sem.at[step],
            recv_sem=recv_sem.at[step],
            device_id=target,
            device_id_type=pl.DeviceIdType.MESH,
        )
        copy.start()
        copies.append(copy)
    own = pltpu.make_async_copy(in_ref if same else in_ref.at[me], out_ref.at[me], local_sem)
    own.start()
    own.wait()
    for copy in copies:
        copy.wait()


def exchange(array, axis, collective_id, stride=1, same=True, space=pltpu.VMEM):
    size = lax.axis_size(axis) // stride
    shape = (size,) + array.shape if same else array.shape
    return pl.pallas_call(
        functools.partial(exchange_kernel, axis, stride, same),
        out_shape=jax.ShapeDtypeStruct(shape, array.dtype),
        in_specs=[pl.BlockSpec(memory_space=space)],
        out_specs=pl.BlockSpec(memory_space=space),
        scratch_shapes=[
            pltpu.SemaphoreType.DMA((size - 1,)),
            pltpu.SemaphoreType.DMA((size - 1,)),
            pltpu.SemaphoreType.DMA,
        ],
        compiler_params=pltpu.CompilerParams(collective_id=collective_id, has_side_effects=True),
    )(array)


def pick_kernel(row_ref, col_ref, keep_ref, in_ref, out_ref):
    keep = keep_ref[pl.program_id(0)] > 0

    @pl.when(keep)
    def _():
        out_ref[0] = in_ref[...]

    @pl.when(jnp.logical_not(keep))
    def _():
        out_ref[...] = jnp.zeros_like(out_ref)


def pick_tiles(dpsi_grad, row_blocks, col_blocks, keep):
    count = row_blocks.shape[0]
    return pl.pallas_call(
        pick_kernel,
        out_shape=jax.ShapeDtypeStruct((count, BS, BS), dpsi_grad.dtype),
        grid_spec=pltpu.PrefetchScalarGridSpec(
            num_scalar_prefetch=3,
            grid=(count,),
            in_specs=[pl.BlockSpec((BS, BS), lambda t, rows, cols, keeps: (rows[t], cols[t]))],
            out_specs=pl.BlockSpec((1, BS, BS), lambda t, rows, cols, keeps: (t, 0, 0)),
        ),
    )(row_blocks, col_blocks, keep, dpsi_grad)


def on_device(x_points, z_points, length_scales, dpsi_grad, block_rows, block_cols, block_count):
    highest = lax.Precision.HIGHEST
    groups_dp = lax.axis_size("dp")
    groups_ind = lax.axis_size("ind")
    dp_index = lax.axis_index("dp")
    ind_index = lax.axis_index("ind")
    owner_ratio = groups_dp // groups_ind
    col_blocks = M // (BS * groups_ind)
    own_blocks = M // (BS * groups_dp)
    dim_count = x_points.shape[0]
    slot_count = block_rows.shape[2]
    row_count = x_points.shape[1] // BS
    slot_ids = jnp.arange(slot_count, dtype=jnp.int32)
    batched_kernel = jax.vmap(wendland, in_axes=(0, 0, None))
    def lane_row(values):
        return jnp.pad(values, (0, 128 - values.shape[0]))[None, :]

    meta = jnp.pad(
        jnp.concatenate(
            [lane_row(block_rows[0, 0]), lane_row(block_cols[0, 0]), lane_row(block_count[0])]
        ),
        ((0, 5), (0, 0)),
    )
    meta_ind = exchange(meta, "ind", 0)
    z_all = exchange(z_points, "ind", 1)
    meta_all = exchange(meta_ind.reshape(groups_ind * 8, 128), "dp", 2)
    meta_all = meta_all.reshape(groups_dp, groups_ind, 8, 128)
    all_count = meta_all[:, :, 2, 0]
    live_all = slot_ids[None, None, :] < all_count[:, :, None]
    all_rows = jnp.where(live_all, meta_all[:, :, 0, :slot_count], 0)
    all_cols = jnp.where(live_all, meta_all[:, :, 1, :slot_count], 0)
    z_blocks = z_all.reshape(groups_ind, dim_count, col_blocks, BS)
    own_mask = slot_ids < block_count[0, 0]
    own_rows = jnp.where(own_mask, block_rows[0, 0], 0)
    own_cols = jnp.where(own_mask, block_cols[0, 0], 0)
    own_live = own_mask.astype(jnp.float32)
    x_own = jnp.transpose(x_points.reshape(dim_count, row_count, BS)[:, own_rows, :], (1, 0, 2))
    my_group = dp_index // owner_ratio
    my_part = dp_index % owner_ratio
    dest_rows = all_rows[:, ind_index, :]
    dest_cols = all_cols[:, ind_index, :]
    source_rows = all_rows[:, my_group, :]
    source_cols = all_cols[:, my_group, :]
    source_live = live_all[:, my_group, :]
    matched = source_live[:, None, :] & (source_rows[:, None, :] == dest_rows[:, :, None])
    found_col = jnp.sum(jnp.where(matched, source_cols[:, None, :], 0), axis=2)
    dest_live = live_all[:, ind_index, :]
    keep = jnp.any(matched, axis=2) & (found_col // own_blocks == my_part) & dest_live
    pick_rows = jnp.where(keep, found_col - my_part * own_blocks, 0)
    pick_cols = jnp.where(keep, dest_cols, 0)

    def pair_first(values):
        return jnp.transpose(
            values.reshape(groups_ind, owner_ratio, slot_count), (1, 0, 2)
        ).reshape(-1)

    outgoing = pick_tiles(
        dpsi_grad,
        pair_first(pick_rows),
        pair_first(pick_cols),
        pair_first(keep.astype(jnp.int32)),
    ).reshape(owner_ratio, groups_ind * slot_count, BS, BS)
    swap = [(index, index ^ 1) for index in range(groups_dp)]
    from_pair = lax.ppermute(outgoing[1 - my_part], "dp", swap)
    combined = (outgoing[my_part] + from_pair).reshape(groups_ind, slot_count, BS, BS)
    grouped = exchange(combined, "dp", 3, stride=owner_ratio, same=False, space=pl.ANY)
    row_tiles = all_rows[dp_index]
    col_tiles = all_cols[dp_index]
    live_tiles = live_all[dp_index]
    near_match = live_tiles[None, :, :] & (row_tiles[None, :, :] == own_rows[:, None, None])
    near_weight = jnp.any(near_match, axis=2).astype(jnp.float32)
    near_local = jnp.sum(jnp.where(near_match, col_tiles[None, :, :], 0), axis=2)
    group_ids = jnp.arange(groups_ind, dtype=jnp.int32)
    z_near = jnp.transpose(
        z_blocks[group_ids[None, :], :, near_local, :], (0, 2, 1, 3)
    ).reshape(slot_count, dim_count, groups_ind * BS)
    kernel, _ = batched_kernel(x_own, z_near, length_scales)
    masked = kernel * jnp.repeat(near_weight, BS, axis=1)[:, None, :]
    dk_local = jnp.einsum(
        "spgk,gskc->spc", masked.reshape(slot_count, BS, groups_ind, BS), grouped, precision=highest
    )
    dk_local = dk_local * own_live[:, None, None]
    z_own = jnp.transpose(z_points.reshape(dim_count, col_blocks, BS)[:, own_cols, :], (1, 0, 2))
    _, slopes = batched_kernel(x_own, z_own, length_scales)
    grad_k = dk_local * slopes
    col_sum = jnp.sum(grad_k, axis=1)
    x_weighted = jnp.einsum("sqn,snm->sqm", x_own, grad_k, precision=highest)
    inverse_square = -2.0 / (length_scales * length_scales)
    z_parts = inverse_square[None, :, None] * (x_weighted - z_own * col_sum[:, None, :])
    scale_terms = []
    for dim_q in range(dim_count):
        offset = x_own[:, dim_q, :, None] - z_own[:, dim_q, None, :]
        scale_terms.append(jnp.sum(grad_k * offset * offset, axis=(1, 2)))
    cube_scale = length_scales * length_scales * length_scales
    scale_parts = (-2.0 / cube_scale)[None, :] * jnp.stack(scale_terms, axis=1)
    part_rows = slot_count * dim_count
    scale_row = jnp.pad(jnp.sum(scale_parts, axis=0), (0, BS - dim_count))[None, :]
    sent = jnp.concatenate([z_parts.reshape(part_rows, BS), scale_row])
    sent = jnp.pad(sent, ((0, -(part_rows + 1) % 8), (0, 0)))
    parts = exchange(sent, "dp", 4)
    scale_sum = jnp.sum(parts[:, part_rows, :128], axis=0)
    scale_all = exchange(jnp.broadcast_to(scale_sum[None, :], (8, 128)), "ind", 5)
    scale_grad = jnp.sum(scale_all[:, 0, :dim_count], axis=0)
    onehot = (
        dest_cols.reshape(-1)[:, None] == jnp.arange(col_blocks, dtype=jnp.int32)[None, :]
    ).astype(jnp.float32)
    z_grad = jnp.einsum(
        "tc,tqb->qcb",
        onehot,
        parts[:, :part_rows, :].reshape(groups_dp * slot_count, dim_count, BS),
        precision=highest,
    ).reshape(dim_count, col_blocks * BS)
    return (dk_local.reshape(1, 1, slot_count, BS, BS), z_grad, scale_grad)


def solution(mesh):
    return jax.shard_map(
        on_device,
        mesh=mesh,
        in_specs=(
            P(None, "dp"),
            P(None, "ind"),
            P(),
            P("dp", "ind"),
            P("dp", "ind", None),
            P("dp", "ind", None),
            P("dp", "ind"),
        ),
        out_specs=(P("dp", "ind", None, None, None), P(None, "ind"), P()),
        check_vma=False,
    )
```

```python
import functools

import jax
import jax.numpy as jnp
from jax import lax
from jax.experimental import pallas as pl
from jax.experimental.pallas import tpu as pltpu
from jax.sharding import PartitionSpec as P

M = 16384
BS = 256
PICKS = 4


def wendland(x_rows, z_cols, length_scales):
    dist_sq = jnp.zeros((x_rows.shape[1], z_cols.shape[1]), x_rows.dtype)
    for dim_q in range(x_rows.shape[0]):
        offset = (x_rows[dim_q][:, None] - z_cols[dim_q][None, :]) / length_scales[dim_q]
        dist_sq = dist_sq + offset * offset
    radius = jnp.sqrt(dist_sq)
    remain = jnp.maximum(1.0 - radius, 0.0)
    remain_cube = remain * remain * remain
    return (remain_cube * remain * (4.0 * radius + 1.0), -10.0 * remain_cube)


def peers_of(axis, stride):
    size = lax.axis_size(axis) // stride
    index = lax.axis_index(axis)
    me = index // stride
    lane = index % stride
    others = []
    for step in range(1, size):
        other = lax.rem(me + step, size)
        others.append((other, {axis: other * stride + lane}))
    return me, others


def exchange_kernel(axis, stride, same, in_ref, out_ref, send_sem, recv_sem, local_sem):
    me, others = peers_of(axis, stride)
    barrier = pltpu.get_barrier_semaphore()
    for _, target in others:
        pl.semaphore_signal(barrier, inc=1, device_id=target, device_id_type=pl.DeviceIdType.MESH)
    pl.semaphore_wait(barrier, len(others))
    copies = []
    for step, (other, target) in enumerate(others):
        copy = pltpu.make_async_remote_copy(
            src_ref=in_ref if same else in_ref.at[other],
            dst_ref=out_ref.at[me],
            send_sem=send_sem.at[step],
            recv_sem=recv_sem.at[step],
            device_id=target,
            device_id_type=pl.DeviceIdType.MESH,
        )
        copy.start()
        copies.append(copy)
    own = pltpu.make_async_copy(in_ref if same else in_ref.at[me], out_ref.at[me], local_sem)
    own.start()
    own.wait()
    for copy in copies:
        copy.wait()


def exchange(array, axis, collective_id, stride=1, same=True, space=pltpu.VMEM):
    size = lax.axis_size(axis) // stride
    shape = (size,) + array.shape if same else array.shape
    return pl.pallas_call(
        functools.partial(exchange_kernel, axis, stride, same),
        out_shape=jax.ShapeDtypeStruct(shape, array.dtype),
        in_specs=[pl.BlockSpec(memory_space=space)],
        out_specs=pl.BlockSpec(memory_space=space),
        scratch_shapes=[
            pltpu.SemaphoreType.DMA((size - 1,)),
            pltpu.SemaphoreType.DMA((size - 1,)),
            pltpu.SemaphoreType.DMA,
        ],
        compiler_params=pltpu.CompilerParams(collective_id=collective_id, has_side_effects=True),
    )(array)


def pick_kernel(has_other, row_ref, col_ref, keep_ref, *refs):
    out_ref = refs[-1]
    for place in range(PICKS):
        keep = keep_ref[pl.program_id(0) * PICKS + place] > 0

        @pl.when(keep)
        def _():
            out_ref[place] = refs[place][...]

        @pl.when(jnp.logical_not(keep))
        def _():
            if has_other:
                out_ref[place] = refs[PICKS][place]
            else:
                out_ref[place] = jnp.zeros_like(out_ref[place])


def pick_tiles(dpsi_grad, row_blocks, col_blocks, keep, other=None):
    count = row_blocks.shape[0]
    stacked = pl.BlockSpec((PICKS, BS, BS), lambda t, rows, cols, keeps: (t, 0, 0))

    def tile_spec(place):
        return pl.BlockSpec(
            (BS, BS),
            lambda t, rows, cols, keeps: (rows[t * PICKS + place], cols[t * PICKS + place]),
        )

    extra = [] if other is None else [other]
    return pl.pallas_call(
        functools.partial(pick_kernel, other is not None),
        out_shape=jax.ShapeDtypeStruct((count, BS, BS), dpsi_grad.dtype),
        grid_spec=pltpu.PrefetchScalarGridSpec(
            num_scalar_prefetch=3,
            grid=(count // PICKS,),
            in_specs=[tile_spec(place) for place in range(PICKS)] + [stacked] * len(extra),
            out_specs=stacked,
        ),
        compiler_params=pltpu.CompilerParams(vmem_limit_bytes=24 * 1024 * 1024),
    )(row_blocks, col_blocks, keep, *([dpsi_grad] * PICKS), *extra)


def on_device(x_points, z_points, length_scales, dpsi_grad, block_rows, block_cols, block_count):
    highest = lax.Precision.HIGHEST
    groups_dp = lax.axis_size("dp")
    groups_ind = lax.axis_size("ind")
    dp_index = lax.axis_index("dp")
    ind_index = lax.axis_index("ind")
    owner_ratio = groups_dp // groups_ind
    col_blocks = M // (BS * groups_ind)
    own_blocks = M // (BS * groups_dp)
    dim_count = x_points.shape[0]
    slot_count = block_rows.shape[2]
    row_count = x_points.shape[1] // BS
    slot_ids = jnp.arange(slot_count, dtype=jnp.int32)
    batched_kernel = jax.vmap(wendland, in_axes=(0, 0, None))
    def lane_row(values):
        return jnp.pad(values, (0, 128 - values.shape[0]))[None, :]

    meta = jnp.pad(
        jnp.concatenate(
            [lane_row(block_rows[0, 0]), lane_row(block_cols[0, 0]), lane_row(block_count[0])]
        ),
        ((0, 5), (0, 0)),
    )
    meta_ind = exchange(meta, "ind", 0)
    z_all = exchange(z_points, "ind", 1)
    meta_all = exchange(meta_ind.reshape(groups_ind * 8, 128), "dp", 2)
    meta_all = meta_all.reshape(groups_dp, groups_ind, 8, 128)
    all_count = meta_all[:, :, 2, 0]
    live_all = slot_ids[None, None, :] < all_count[:, :, None]
    all_rows = jnp.where(live_all, meta_all[:, :, 0, :slot_count], 0)
    all_cols = jnp.where(live_all, meta_all[:, :, 1, :slot_count], 0)
    z_blocks = z_all.reshape(groups_ind, dim_count, col_blocks, BS)
    own_mask = slot_ids < block_count[0, 0]
    own_rows = jnp.where(own_mask, block_rows[0, 0], 0)
    own_cols = jnp.where(own_mask, block_cols[0, 0], 0)
    own_live = own_mask.astype(jnp.float32)
    x_own = jnp.transpose(x_points.reshape(dim_count, row_count, BS)[:, own_rows, :], (1, 0, 2))
    my_group = dp_index // owner_ratio
    my_part = dp_index % owner_ratio
    dest_rows = all_rows[:, ind_index, :]
    dest_cols = all_cols[:, ind_index, :]
    source_rows = all_rows[:, my_group, :]
    source_cols = all_cols[:, my_group, :]
    source_live = live_all[:, my_group, :]
    matched = source_live[:, None, :] & (source_rows[:, None, :] == dest_rows[:, :, None])
    found_col = jnp.sum(jnp.where(matched, source_cols[:, None, :], 0), axis=2)
    dest_live = live_all[:, ind_index, :]
    keep = jnp.any(matched, axis=2) & (found_col // own_blocks == my_part) & dest_live
    pick_rows = jnp.where(keep, found_col - my_part * own_blocks, 0)
    pick_cols = jnp.where(keep, dest_cols, 0)

    def pair_first(values):
        return jnp.transpose(
            values.reshape(groups_ind, owner_ratio, slot_count), (1, 0, 2)
        ).reshape(owner_ratio, -1)

    pick_lists = (pair_first(pick_rows), pair_first(pick_cols), pair_first(keep.astype(jnp.int32)))
    outgoing = pick_tiles(dpsi_grad, *[values[1 - my_part] for values in pick_lists])
    swap = [(index, index ^ 1) for index in range(groups_dp)]
    from_pair = lax.ppermute(outgoing, "dp", swap)
    combined = pick_tiles(dpsi_grad, *[values[my_part] for values in pick_lists], from_pair)
    combined = combined.reshape(groups_ind, slot_count, BS, BS)
    grouped = exchange(combined, "dp", 3, stride=owner_ratio, same=False, space=pl.ANY)
    row_tiles = all_rows[dp_index]
    col_tiles = all_cols[dp_index]
    live_tiles = live_all[dp_index]
    near_match = live_tiles[None, :, :] & (row_tiles[None, :, :] == own_rows[:, None, None])
    near_weight = jnp.any(near_match, axis=2).astype(jnp.float32)
    near_local = jnp.sum(jnp.where(near_match, col_tiles[None, :, :], 0), axis=2)
    group_ids = jnp.arange(groups_ind, dtype=jnp.int32)
    z_near = jnp.transpose(
        z_blocks[group_ids[None, :], :, near_local, :], (0, 2, 1, 3)
    ).reshape(slot_count, dim_count, groups_ind * BS)
    kernel, _ = batched_kernel(x_own, z_near, length_scales)
    masked = kernel * jnp.repeat(near_weight, BS, axis=1)[:, None, :]
    dk_local = jnp.einsum(
        "spgk,gskc->spc", masked.reshape(slot_count, BS, groups_ind, BS), grouped, precision=highest
    )
    dk_local = dk_local * own_live[:, None, None]
    z_own = jnp.transpose(z_points.reshape(dim_count, col_blocks, BS)[:, own_cols, :], (1, 0, 2))
    _, slopes = batched_kernel(x_own, z_own, length_scales)
    grad_k = dk_local * slopes
    col_sum = jnp.sum(grad_k, axis=1)
    x_weighted = jnp.einsum("sqn,snm->sqm", x_own, grad_k, precision=highest)
    inverse_square = -2.0 / (length_scales * length_scales)
    z_parts = inverse_square[None, :, None] * (x_weighted - z_own * col_sum[:, None, :])
    scale_terms = []
    for dim_q in range(dim_count):
        offset = x_own[:, dim_q, :, None] - z_own[:, dim_q, None, :]
        scale_terms.append(jnp.sum(grad_k * offset * offset, axis=(1, 2)))
    cube_scale = length_scales * length_scales * length_scales
    scale_parts = (-2.0 / cube_scale)[None, :] * jnp.stack(scale_terms, axis=1)
    part_rows = slot_count * dim_count
    scale_row = jnp.pad(jnp.sum(scale_parts, axis=0), (0, BS - dim_count))[None, :]
    sent = jnp.concatenate([z_parts.reshape(part_rows, BS), scale_row])
    sent = jnp.pad(sent, ((0, -(part_rows + 1) % 8), (0, 0)))
    parts = exchange(sent, "dp", 4)
    scale_sum = jnp.sum(parts[:, part_rows, :128], axis=0)
    scale_all = exchange(jnp.broadcast_to(scale_sum[None, :], (8, 128)), "ind", 5)
    scale_grad = jnp.sum(scale_all[:, 0, :dim_count], axis=0)
    onehot = (
        dest_cols.reshape(-1)[:, None] == jnp.arange(col_blocks, dtype=jnp.int32)[None, :]
    ).astype(jnp.float32)
    z_grad = jnp.einsum(
        "tc,tqb->qcb",
        onehot,
        parts[:, :part_rows, :].reshape(groups_dp * slot_count, dim_count, BS),
        precision=highest,
    ).reshape(dim_count, col_blocks * BS)
    return (dk_local.reshape(1, 1, slot_count, BS, BS), z_grad, scale_grad)


def solution(mesh):
    return jax.shard_map(
        on_device,
        mesh=mesh,
        in_specs=(
            P(None, "dp"),
            P(None, "ind"),
            P(),
            P("dp", "ind"),
            P("dp", "ind", None),
            P("dp", "ind", None),
            P("dp", "ind"),
        ),
        out_specs=(P("dp", "ind", None, None, None), P(None, "ind"), P()),
        check_vma=False,
    )
```
